256 devices in a mesh: basis: 32 (over x, z), tile: 8 (over y, core).
Axes of the slice: x: 4, y: 4, z: 8, core: 2. Of those that a mesh axis runs over, the one named last changes fastest.
Arguments:
- lower_vectors: bfloat16 [1536, 256, 256], P('basis'), may hold values from -0.005859375 to 0.005859375
- upper_vectors: bfloat16 [1024, 256, 1024], P('basis', None, 'tile'), may hold values from -6 to 6
- dipole_vib: bfloat16 [3, 256, 256], replicated, may hold values from -0.375 to 0.375
- rot_factor: float32 [1536, 3], P('basis'), may hold values from 0.5 to 1.5
- coupling: int32 [1536, 3], P('basis'), may hold values 0 or 1
- lower_sizes: int32 [1536], P('basis'), may hold values from 128 to 256
- upper_sizes: int32 [1024], P('basis'), may hold values from 128 to 256
- lower_range: int32 [32, 2], P('basis'), may hold values from 0 to 1024, as said below
Outputs:
- strength: float32 [256, 1024], P('basis', 'tile')
- average: float32 [256], P('basis')
The draws below stay inside these ranges and needn't reach their ends.
Inputs may be any that keep to these rules, and one draw needn't show every extreme that they name: `lower_range`: the ranges are contiguous in device order and cover 0 to 1024; device j starts within 8 blocks of j * 32 (device 0 at 0); at least one device holds exactly 48 blocks, and none holds more.
All inputs are finite; a program needn't handle non-finite values. No bound on the sum of `coupling` on one device may be relied on, other than what follows from the above.
Results may differ from the reference program's by a relative error of at most 0.0065.
Values may be sent and summed in bfloat16 or wider, within the bound.
No kernel may reach another device: no remote copies, remote signals or barrier semaphores. Data moves between devices by JAX's collectives and lax.ppermute only.
A program may use at most 128 MiB of HBM per device.

```python
import jax
import jax.numpy as jnp
from jax import lax

BR = 256
NLOW = 256
NUP = 1024
BLK_DEV = 32
SLOTS = 48
NBLK = 1024
LSLOTS = 1536


def draw_lower_range(key, part):
    key = jax.random.fold_in(key, 7)
    devices = NBLK // BLK_DEV
    spread = BLK_DEV // 4
    first_key, pick_key = jax.random.split(key)
    offsets = jax.random.randint(first_key, (devices + 1,), -spread, spread + 1)
    chosen = jax.random.randint(pick_key, (), 1, devices - 1)
    indices = jnp.arange(devices + 1, dtype=jnp.int32)
    offsets = jnp.where(indices == chosen, -spread, offsets)
    offsets = jnp.where(indices == chosen + 1, spread, offsets)
    offsets = jnp.where((indices == 0) | (indices == devices), 0, offsets)
    bounds = indices * BLK_DEV + offsets
    return jnp.stack([bounds[:-1], bounds[1:]], axis=1).astype(jnp.int32)


def touch_ends(drawn, stream_key, least, high):
    spot = [jax.random.randint(jax.random.fold_in(stream_key, axis), (), 0, length) for axis, length in enumerate(drawn.shape)]
    widest = drawn.shape.index(max(drawn.shape))
    next_to = spot[:widest] + [(spot[widest] + 1) % drawn.shape[widest]] + spot[widest + 1:]
    return drawn.at[tuple(spot)].set(least).at[tuple(next_to)].set(high)


def level_of(rng, shape, shards, smallest, largest):
    gain = 1.0
    for position, parts in shards:
        draws = jax.random.uniform(jax.random.fold_in(jax.random.fold_in(rng, 6), position), (parts,), jnp.float32, smallest / len(shards), largest / len(shards))
        gain = gain * jnp.repeat(jnp.exp(draws), shape[position] // parts).reshape((-1,) + (1,) * (len(shape) - 1 - position))
    return gain


def gaussian(own_key, dims, scale, bound, cuts=(), kind=jnp.bfloat16):
    gain = level_of(own_key, dims, cuts, -0.22, 0.18) if cuts else 1.0
    entries = jax.random.normal(own_key, dims, jnp.float32) * scale * gain
    return jnp.minimum(jnp.maximum(entries, -bound), bound).astype(kind)


def setup_inputs(seed: int = 0) -> dict:
    arg_keys = jax.random.split(jax.random.key(seed), 9)
    lower_vectors = gaussian(arg_keys[0], (LSLOTS, BR, NLOW), (4 * NBLK * BR) ** -0.5, 0.005859375, ((0, 32),))
    upper_vectors = gaussian(arg_keys[1], (NBLK, BR, NUP), 1.0, 6.0, ((0, 32), (2, 8)))
    dipole_vib = gaussian(arg_keys[2], (3, BR, BR), BR ** -0.5, 0.375)
    rot_factor = jnp.clip(0.5 + 1.0 * jax.random.uniform(arg_keys[3], (LSLOTS, 3), jnp.float32) ** level_of(arg_keys[3], (LSLOTS, 3), ((0, 32),), -0.2, 0.2), 0.5, 1.5)
    coupling = touch_ends((jax.random.randint(arg_keys[4], (LSLOTS, 3), 0, 4) < 3).astype(jnp.int32), jax.random.fold_in(arg_keys[4], 1), 0, 1)
    lower_sizes = touch_ends(jax.random.randint(arg_keys[5], (LSLOTS,), BR // 2, BR + 1), jax.random.fold_in(arg_keys[5], 1), BR // 2, BR).astype(jnp.int32)
    upper_sizes = touch_ends(jax.random.randint(arg_keys[6], (NBLK,), BR // 2, BR + 1), jax.random.fold_in(arg_keys[6], 1), BR // 2, BR).astype(jnp.int32)
    lower_range = draw_lower_range(jax.random.fold_in(arg_keys[8], 71), 0)
    return dict(lower_vectors=lower_vectors, upper_vectors=upper_vectors, dipole_vib=dipole_vib, rot_factor=rot_factor, coupling=coupling, lower_sizes=lower_sizes, upper_sizes=upper_sizes, lower_range=lower_range)


def reference(lower_vectors, upper_vectors, dipole_vib, rot_factor, coupling, lower_sizes, upper_sizes, lower_range):
    starts = lower_range[:, 0]
    row_ids = jnp.arange(BR, dtype=jnp.int32)
    vibration = dipole_vib.astype(jnp.float32)
    highest = lax.Precision.HIGHEST

    def accumulate(moment, block):
        device = (jnp.sum((starts <= block).astype(jnp.int32)) - 1).astype(jnp.int32)
        slot_index = (device * SLOTS + block - starts[device]).astype(jnp.int32)
        lower_block = lax.dynamic_index_in_dim(lower_vectors, slot_index, 0, keepdims=False).astype(jnp.float32)
        live_rows = row_ids < lower_sizes[slot_index]
        lower_block = jnp.where(live_rows[:, None], lower_block, jnp.float32(0.0))
        image_sum = jnp.zeros((BR, NUP), jnp.float32)
        for coupled in range(3):
            target = block + coupled - 1
            inside = (target >= 0) & (target < NBLK)
            clamped = jnp.clip(target, 0, NBLK - 1).astype(jnp.int32)
            upper_block = lax.dynamic_index_in_dim(upper_vectors, clamped, 0, keepdims=False).astype(jnp.float32)
            keep = (row_ids < upper_sizes[clamped]) & inside
            upper_block = jnp.where(keep[:, None], upper_block, jnp.float32(0.0))
            factor = rot_factor[slot_index, coupled] * coupling[slot_index, coupled].astype(jnp.float32)
            image_sum = image_sum + factor * jnp.dot(vibration[coupled], upper_block, precision=highest)
        rounded = lax.optimization_barrier(image_sum.astype(jnp.bfloat16)).astype(jnp.float32)
        moment = moment + jnp.dot(lower_block.T, rounded, precision=highest)
        return moment, None

    moment, ignored = lax.scan(accumulate, jnp.zeros((NLOW, NUP), jnp.float32), jnp.arange(NBLK, dtype=jnp.int32))
    strength = moment * moment
    return strength, jnp.sum(strength, axis=1) / NUP
```

```python
import functools

import jax
import jax.numpy as jnp
from jax import lax
from jax.experimental import pallas as pl
from jax.experimental.pallas import tpu as pltpu
from jax.sharding import PartitionSpec as P

NUP = 1024
SHIFT = 8
MARGIN = SHIFT + 1
GROUP = 8
VMEM_BYTES = 48 * 1024 * 1024
BF16 = jnp.bfloat16
F32 = jnp.float32


def vmem_spec():
    return pl.BlockSpec(memory_space=pltpu.VMEM)


def smem_spec():
    return pl.BlockSpec(memory_space=pltpu.SMEM)


def edges_kernel(sizes, upper, low, high, sems):
    blocks, rows, _ = upper.shape
    margin = low.shape[0]
    copies = [
        pltpu.make_async_copy(upper.at[pl.ds(blocks - margin, margin)], low, sems.at[0]),
        pltpu.make_async_copy(upper.at[pl.ds(0, margin)], high, sems.at[1]),
    ]
    for copy in copies:
        copy.start()
    row_ids = lax.broadcasted_iota(jnp.int32, low.shape[1:], 0)
    for copy, out, first in zip(copies, (low, high), (blocks - margin, 0)):
        copy.wait()
        for block in range(margin):
            out[block] = jnp.where(
                row_ids < sizes[first + block], out[block], jnp.zeros((), BF16)
            )


def edges(upper_sizes, upper_vectors):
    blocks, rows, columns = upper_vectors.shape
    shape = pltpu.VMEM((MARGIN, rows, columns), BF16)
    return pl.pallas_call(
        edges_kernel,
        out_shape=(shape, shape),
        in_specs=[smem_spec(), pl.BlockSpec(memory_space=pl.ANY)],
        out_specs=(vmem_spec(), vmem_spec()),
        scratch_shapes=[pltpu.SemaphoreType.DMA((2,))],
        name="edges",
    )(upper_sizes, upper_vectors)


def inner_kernel(
    first_ref,
    range_ref,
    rot,
    coupling,
    lower_sizes,
    upper_sizes,
    lower,
    upper,
    dipole,
    outer,
    partial,
    images,
    carry,
):
    step = pl.program_id(0)
    blocks = upper.shape[0]
    rows, states = lower.shape[1], lower.shape[2]
    start = range_ref[0, 0]
    count = range_ref[0, 1] - start
    base = start - first_ref[0] + MARGIN
    row_ids = lax.broadcasted_iota(jnp.int32, (rows, states), 0)

    @pl.when(step == 0)
    def _():
        carry[...] = jnp.zeros_like(carry)
        for index in range(images.shape[0]):
            images[index] = jnp.zeros(images.shape[1:], BF16)

    def one(slot, _):
        local = slot - step * GROUP
        live = jnp.where(row_ids < lower_sizes[slot], lower[local], jnp.zeros((), BF16))
        turned = live.T
        parts = []
        for d in range(3):
            factor = rot[d, slot] * coupling[d, slot].astype(F32)
            parts.append(factor * jnp.dot(turned, dipole[d], preferred_element_type=F32))
        images[base + slot - 1] = (carry[0] + parts[0]).astype(BF16)
        carry[0] = carry[1] + parts[1]
        carry[1] = parts[2]
        return 0

    lax.fori_loop(step * GROUP, jnp.minimum(step * GROUP + GROUP, count), one, 0)

    @pl.when(step == pl.num_programs(0) - 1)
    def _():
        images[base + count - 1] = carry[0].astype(BF16)
        images[base + count] = carry[1].astype(BF16)
        up_ids = lax.broadcasted_iota(jnp.int32, upper.shape[1:], 0)
        partial[...] = jnp.zeros_like(partial)

        def mine(block, _):
            live = jnp.where(up_ids < upper_sizes[block], upper[block], jnp.zeros((), BF16))
            partial[...] += jnp.dot(images[block + MARGIN], live, preferred_element_type=F32)
            return 0

        lax.fori_loop(0, blocks, mine, 0)
        for index in range(MARGIN):
            outer[index] = images[index]
            outer[MARGIN + index] = images[MARGIN + blocks + index]


def inner(first, lower_range, rot, coupling, lower_sizes, upper_sizes, lower, upper, dipole):
    slots, rows, states = lower.shape
    blocks, _, columns = upper.shape
    return pl.pallas_call(
        inner_kernel,
        grid=(slots // GROUP,),
        out_shape=(
            pltpu.VMEM((2 * MARGIN, states, rows), BF16),
            pltpu.VMEM((states, columns), F32),
        ),
        in_specs=[smem_spec() for _ in range(6)]
        + [
            pl.BlockSpec((GROUP, rows, states), lambda step: (step, 0, 0)),
            vmem_spec(),
            vmem_spec(),
        ],
        out_specs=(vmem_spec(), vmem_spec()),
        scratch_shapes=[
            pltpu.VMEM((blocks + 2 * MARGIN, states, rows), BF16),
            pltpu.VMEM((2, states, rows), F32),
        ],
        compiler_params=pltpu.CompilerParams(vmem_limit_bytes=VMEM_BYTES),
        name="inner",
    )(first, lower_range, rot, coupling, lower_sizes, upper_sizes, lower, upper, dipole)


def outer_kernel(low, high, images, partial, out):
    total = partial[...]
    margin = low.shape[0]
    for index in range(margin):
        total += jnp.dot(images[index], low[index], preferred_element_type=F32)
    for index in range(margin):
        total += jnp.dot(images[margin + index], high[index], preferred_element_type=F32)
    out[...] = total.reshape(out.shape).astype(out.dtype)


def outer(low, high, images, partial, parts):
    states, columns = partial.shape
    return pl.pallas_call(
        outer_kernel,
        out_shape=pltpu.VMEM((parts, states // parts, columns), BF16),
        in_specs=[vmem_spec() for _ in range(4)],
        out_specs=vmem_spec(),
        compiler_params=pltpu.CompilerParams(vmem_limit_bytes=VMEM_BYTES),
        name="outer",
    )(low, high, images, partial)


def square_kernel(received, strength, sums):
    moment = jnp.sum(received[...].astype(F32), axis=0)
    squared = moment * moment
    strength[...] = squared
    sums[...] = jnp.broadcast_to(jnp.sum(squared, axis=1, keepdims=True)[None], sums.shape)


def square(received, tiles):
    _, band, columns = received.shape
    return pl.pallas_call(
        square_kernel,
        out_shape=(
            jax.ShapeDtypeStruct((band, columns), F32),
            pltpu.VMEM((tiles, band, 128), F32),
        ),
        in_specs=[vmem_spec()],
        out_specs=(vmem_spec(), vmem_spec()),
        name="square",
    )(received)


def shards(
    lower_vectors,
    upper_vectors,
    dipole_vib,
    rot_factor,
    coupling,
    lower_sizes,
    upper_sizes,
    lower_range,
):
    parts = lax.axis_size("basis")
    tiles = lax.axis_size("tile")
    blocks = upper_vectors.shape[0]
    first = (lax.axis_index("basis") * blocks).astype(jnp.int32).reshape(1)
    forward = [(i, i + 1) for i in range(parts - 1)]
    backward = [(target, source) for source, target in forward]
    last_blocks, first_blocks = edges(upper_sizes, upper_vectors)
    low = lax.ppermute(last_blocks, "basis", forward)
    high = lax.ppermute(first_blocks, "basis", backward)
    images, partial = inner(
        first,
        lower_range,
        rot_factor.T,
        coupling.T,
        lower_sizes,
        upper_sizes,
        lower_vectors,
        upper_vectors,
        dipole_vib,
    )
    mine = outer(low, high, images, partial, parts)
    received = lax.all_to_all(mine, "basis", 0, 0, tiled=True)
    strength, sums = square(received, tiles)
    gathered = lax.all_to_all(sums, "tile", 0, 0, tiled=True)
    average = jnp.sum(gathered[:, :, 0], axis=0) / NUP
    return (strength, average)


def solution(mesh):
    in_specs = (
        P("basis", None, None),
        P("basis", None, "tile"),
        P(),
        P("basis", None),
        P("basis", None),
        P("basis"),
        P("basis"),
        P("basis", None),
    )
    out_specs = (P("basis", "tile"), P("basis"))
    return jax.shard_map(shards, mesh=mesh, in_specs=in_specs, out_specs=out_specs, check_vma=False)
```

```python
import jax
import jax.numpy as jnp
from jax import lax
from jax.experimental import pallas as pl
from jax.experimental.pallas import tpu as pltpu
from jax.sharding import PartitionSpec as P

NUP = 1024
SHIFT = 8
MARGIN = SHIFT + 1
CHUNK = 12
AHEAD = 2
LEAST = 128
VMEM_BYTES = 28 * 1024 * 1024
BF16 = jnp.bfloat16
F32 = jnp.float32


def vmem_spec():
    return pl.BlockSpec(memory_space=pltpu.VMEM)


def smem_spec():
    return pl.BlockSpec(memory_space=pltpu.SMEM)


def any_spec():
    return pl.BlockSpec(memory_space=pl.ANY)


def in_hbm(array):
    return pltpu.with_memory_space_constraint(array, pltpu.HBM)


def in_vmem(array):
    return pltpu.with_memory_space_constraint(array, pltpu.VMEM)


def edges_kernel(sizes_hbm, upper, low, high, sizes, sems):
    blocks, rows, columns = upper.shape
    margin = low.shape[0]
    copies = [
        pltpu.make_async_copy(upper.at[pl.ds(blocks - margin, margin)], low, sems.at[0]),
        pltpu.make_async_copy(upper.at[pl.ds(0, margin)], high, sems.at[1]),
    ]
    known = pltpu.make_async_copy(sizes_hbm, sizes, sems.at[2])
    known.start()
    for copy in copies:
        copy.start()
    row_ids = LEAST + lax.broadcasted_iota(jnp.int32, (rows - LEAST, columns), 0)
    known.wait()
    for copy, out, first in zip(copies, (low, high), (blocks - margin, 0)):
        copy.wait()
        for block in range(margin):
            out[block, LEAST:] = jnp.where(
                row_ids < sizes[first + block], out[block, LEAST:], jnp.zeros((), BF16)
            )


def edges(upper_sizes, upper_vectors):
    blocks, rows, columns = upper_vectors.shape
    shape = pltpu.VMEM((MARGIN, rows, columns), BF16)
    return pl.pallas_call(
        edges_kernel,
        out_shape=(shape, shape),
        in_specs=[any_spec(), any_spec()],
        out_specs=(vmem_spec(), vmem_spec()),
        scratch_shapes=[
            pltpu.SMEM((blocks,), jnp.int32),
            pltpu.SemaphoreType.DMA((3,)),
        ],
        name="edges",
    )(in_hbm(upper_sizes), in_hbm(upper_vectors))


def masked(block, size):
    rows, columns = block.shape
    row_ids = LEAST + lax.broadcasted_iota(jnp.int32, (rows - LEAST, columns), 0)
    tail = jnp.where(row_ids < size, block[LEAST:], jnp.zeros((), BF16))
    return jnp.concatenate([block[:LEAST], tail], axis=0)


def inner_kernel(
    first_ref,
    range_ref,
    rot,
    coupling,
    lower_sizes,
    upper_sizes,
    lower_hbm,
    upper_hbm,
    dipole_hbm,
    outer,
    partial,
    images,
    turned,
    lower,
    upper,
    dipole,
    sems,
):
    slots, rows, states = lower.shape
    blocks, _, columns = upper.shape
    start = range_ref[0, 0]
    count = range_ref[0, 1] - start
    base = start - first_ref[0] + MARGIN
    chunks = slots // CHUNK
    copies = [
        pltpu.make_async_copy(
            lower_hbm.at[pl.ds(chunk * CHUNK, CHUNK)],
            lower.at[pl.ds(chunk * CHUNK, CHUNK)],
            sems.at[chunk],
        )
        for chunk in range(chunks)
    ]
    copies.append(pltpu.make_async_copy(upper_hbm, upper, sems.at[chunks]))
    first_copy = pltpu.make_async_copy(dipole_hbm, dipole, sems.at[chunks + 1])
    first_copy.start()
    for copy in copies[:AHEAD]:
        copy.start()
    for index in range(2 * MARGIN):
        images[index] = jnp.zeros((rows, states), BF16)
    first_copy.wait()
    for d in range(3):
        turned[d] = dipole[d].T
    nearer = jnp.zeros((rows, states), F32)
    further = jnp.zeros((rows, states), F32)
    for slot in range(slots):
        if slot % CHUNK == 0:
            chunk = slot // CHUNK
            copies[chunk].wait()
            if chunk + AHEAD < len(copies):
                copies[chunk + AHEAD].start()
        live = masked(lower[slot], lower_sizes[slot])
        parts = []
        for d in range(3):
            factor = rot[d, slot] * coupling[d, slot].astype(F32)
            factor = jnp.where(slot < count, factor, 0.0)
            parts.append(factor * jnp.dot(turned[d], live, preferred_element_type=F32))
        images[base + (slot - 1)] = (nearer + parts[0]).astype(BF16)
        nearer = further + parts[1]
        further = parts[2]
    images[base + (slots - 1)] = nearer.astype(BF16)
    images[base + slots] = further.astype(BF16)
    for chunk in range(chunks, len(copies)):
        copies[chunk].wait()
    total = jnp.zeros((columns, states), F32)
    for block in range(blocks):
        live = masked(upper[block], upper_sizes[block])
        total += jnp.dot(live.T, images[MARGIN + block], preferred_element_type=F32)
    partial[...] = total.T
    for index in range(MARGIN):
        outer[index] = images[index].T
        outer[MARGIN + index] = images[MARGIN + blocks + index].T


def inner(first, lower_range, rot, coupling, lower_sizes, upper_sizes, lower, upper, dipole):
    slots, rows, states = lower.shape
    blocks, _, columns = upper.shape
    small = [in_hbm(a) for a in (lower_range, rot, coupling, lower_sizes, upper_sizes)]
    return pl.pallas_call(
        inner_kernel,
        out_shape=(
            pltpu.VMEM((2 * MARGIN, states, rows), BF16),
            pltpu.VMEM((states, columns), F32),
        ),
        in_specs=[smem_spec() for _ in range(6)] + [any_spec() for _ in range(3)],
        out_specs=(vmem_spec(), vmem_spec()),
        scratch_shapes=[
            pltpu.VMEM((slots + 2 * MARGIN + 2, rows, states), BF16),
            pltpu.VMEM((3, rows, rows), BF16),
            pltpu.VMEM(lower.shape, BF16),
            pltpu.VMEM(upper.shape, BF16),
            pltpu.VMEM(dipole.shape, BF16),
            pltpu.SemaphoreType.DMA((slots // CHUNK + 2,)),
        ],
        compiler_params=pltpu.CompilerParams(vmem_limit_bytes=VMEM_BYTES),
        name="inner",
    )(first, *small, in_hbm(lower), in_hbm(upper), in_hbm(dipole))


def outer_kernel(low, high, images, partial, out):
    total = partial[...]
    margin = low.shape[0]
    for index in range(margin):
        total += jnp.dot(images[index], low[index], preferred_element_type=F32)
    for index in range(margin):
        total += jnp.dot(images[margin + index], high[index], preferred_element_type=F32)
    out[...] = total.reshape(out.shape).astype(out.dtype)


def outer(low, high, images, partial, parts):
    states, columns = partial.shape
    return pl.pallas_call(
        outer_kernel,
        out_shape=pltpu.VMEM((parts, states // parts, columns), BF16),
        in_specs=[vmem_spec() for _ in range(4)],
        out_specs=vmem_spec(),
        compiler_params=pltpu.CompilerParams(vmem_limit_bytes=VMEM_BYTES),
        name="outer",
    )(in_vmem(low), in_vmem(high), images, partial)


def square_kernel(received, strength, sums):
    moment = jnp.sum(received[...].astype(F32), axis=0)
    squared = moment * moment
    strength[...] = squared
    row = jnp.sum(squared.T, axis=0, keepdims=True) * (1.0 / NUP)
    sums[...] = jnp.broadcast_to(row[None], sums.shape)


def square(received, tiles):
    _, band, columns = received.shape
    return pl.pallas_call(
        square_kernel,
        out_shape=(
            pltpu.VMEM((band, columns), F32),
            pltpu.VMEM((tiles, 1, band), F32),
        ),
        in_specs=[vmem_spec()],
        out_specs=(vmem_spec(), vmem_spec()),
        name="square",
    )(in_vmem(received))


def shards(
    lower_vectors,
    upper_vectors,
    dipole_vib,
    rot_factor,
    coupling,
    lower_sizes,
    upper_sizes,
    lower_range,
):
    parts = lax.axis_size("basis")
    tiles = lax.axis_size("tile")
    blocks = upper_vectors.shape[0]
    first = (lax.axis_index("basis") * blocks).astype(jnp.int32).reshape(1)
    forward = [(i, i + 1) for i in range(parts - 1)]
    backward = [(target, source) for source, target in forward]
    last_blocks, first_blocks = edges(upper_sizes, upper_vectors)
    low = lax.ppermute(last_blocks, "basis", forward)
    high = lax.ppermute(first_blocks, "basis", backward)
    images, partial = inner(
        first,
        lower_range,
        rot_factor.T,
        coupling.T,
        lower_sizes,
        upper_sizes,
        lower_vectors,
        upper_vectors,
        dipole_vib,
    )
    mine = outer(low, high, images, partial, parts)
    received = lax.all_to_all(mine, "basis", 0, 0, tiled=True)
    strength, sums = square(received, tiles)
    gathered = lax.all_to_all(sums, "tile", 0, 0, tiled=True)
    average = jnp.sum(gathered[:, 0, :], axis=0)
    return (strength, average)


def solution(mesh):
    in_specs = (
        P("basis", None, None),
        P("basis", None, "tile"),
        P(),
        P("basis", None),
        P("basis", None),
        P("basis"),
        P("basis"),
        P("basis", None),
    )
    out_specs = (P("basis", "tile"), P("basis"))
    return jax.shard_map(shards, mesh=mesh, in_specs=in_specs, out_specs=out_specs, check_vma=False)
```

```python
import functools

import jax
import jax.numpy as jnp
from jax import lax
from jax.experimental import pallas as pl
from jax.experimental.pallas import tpu as pltpu
from jax.sharding import PartitionSpec as P

NUP = 1024
SHIFT = 8
MARGIN = SHIFT + 1
CHUNK = 12
AHEAD = 2
LEAST = 128
VMEM_BYTES = 28 * 1024 * 1024
BF16 = jnp.bfloat16
F32 = jnp.float32


def vmem_spec():
    return pl.BlockSpec(memory_space=pltpu.VMEM)


def smem_spec():
    return pl.BlockSpec(memory_space=pltpu.SMEM)


def any_spec():
    return pl.BlockSpec(memory_space=pl.ANY)


def in_hbm(array):
    return pltpu.with_memory_space_constraint(array, pltpu.HBM)


def in_vmem(array):
    return pltpu.with_memory_space_constraint(array, pltpu.VMEM)


def edges_kernel(sizes_hbm, upper, low, high, sizes, sems):
    blocks, rows, columns = upper.shape
    margin = low.shape[0]
    copies = [
        pltpu.make_async_copy(upper.at[pl.ds(blocks - margin, margin)], low, sems.at[0]),
        pltpu.make_async_copy(upper.at[pl.ds(0, margin)], high, sems.at[1]),
    ]
    known = pltpu.make_async_copy(sizes_hbm, sizes, sems.at[2])
    known.start()
    for copy in copies:
        copy.start()
    row_ids = LEAST + lax.broadcasted_iota(jnp.int32, (rows - LEAST, columns), 0)
    known.wait()
    for copy, out, first in zip(copies, (low, high), (blocks - margin, 0)):
        copy.wait()
        for block in range(margin):
            out[block, LEAST:] = jnp.where(
                row_ids < sizes[first + block], out[block, LEAST:], jnp.zeros((), BF16)
            )


def edges(upper_sizes, upper_vectors):
    blocks, rows, columns = upper_vectors.shape
    shape = pltpu.VMEM((MARGIN, rows, columns), BF16)
    return pl.pallas_call(
        edges_kernel,
        out_shape=(shape, shape),
        in_specs=[any_spec(), any_spec()],
        out_specs=(vmem_spec(), vmem_spec()),
        scratch_shapes=[
            pltpu.SMEM((blocks,), jnp.int32),
            pltpu.SemaphoreType.DMA((3,)),
        ],
        name="edges",
    )(in_hbm(upper_sizes), in_hbm(upper_vectors))


def masked(block, size):
    rows, columns = block.shape
    row_ids = LEAST + lax.broadcasted_iota(jnp.int32, (rows - LEAST, columns), 0)
    tail = jnp.where(row_ids < size, block[LEAST:], jnp.zeros((), BF16))
    return jnp.concatenate([block[:LEAST], tail], axis=0)


def inner_kernel(
    total_blocks,
    first_ref,
    range_ref,
    rot,
    coupling,
    lower_sizes,
    upper_sizes,
    lower_hbm,
    upper_hbm,
    dipole_hbm,
    outer,
    partial,
    images,
    turned,
    lower,
    upper,
    dipole,
    sems,
):
    slots, rows, states = lower.shape
    blocks, _, columns = upper.shape
    start = range_ref[0, 0]
    count = range_ref[0, 1] - start
    base = start - first_ref[0] + MARGIN
    chunks = slots // CHUNK
    copies = [
        pltpu.make_async_copy(
            lower_hbm.at[pl.ds(chunk * CHUNK, CHUNK)],
            lower.at[pl.ds(chunk * CHUNK, CHUNK)],
            sems.at[chunk],
        )
        for chunk in range(chunks)
    ]
    copies.append(pltpu.make_async_copy(upper_hbm, upper, sems.at[chunks]))
    first_copy = pltpu.make_async_copy(dipole_hbm, dipole, sems.at[chunks + 1])
    first_copy.start()
    for copy in copies[:AHEAD]:
        copy.start()
    for index in range(2 * MARGIN):
        images[index] = jnp.zeros((rows, states), BF16)
    first_copy.wait()
    for d in range(3):
        turned[d] = dipole[d].T
    nearer = jnp.zeros((rows, states), F32)
    further = jnp.zeros((rows, states), F32)
    for slot in range(slots):
        if slot % CHUNK == 0:
            chunk = slot // CHUNK
            copies[chunk].wait()
            if chunk + AHEAD < len(copies):
                copies[chunk + AHEAD].start()
        live = masked(lower[slot], lower_sizes[slot])
        parts = []
        for d in range(3):
            factor = rot[d, slot] * coupling[d, slot].astype(F32)
            target = start + (slot + d - 1)
            there = (slot < count) & (target >= 0) & (target < total_blocks)
            factor = jnp.where(there, factor, 0.0)
            parts.append(factor * jnp.dot(turned[d], live, preferred_element_type=F32))
        images[base + (slot - 1)] = (nearer + parts[0]).astype(BF16)
        nearer = further + parts[1]
        further = parts[2]
    images[base + (slots - 1)] = nearer.astype(BF16)
    images[base + slots] = further.astype(BF16)
    for chunk in range(chunks, len(copies)):
        copies[chunk].wait()
    total = jnp.zeros((columns, states), F32)
    for block in range(blocks):
        live = masked(upper[block], upper_sizes[block])
        total += jnp.dot(live.T, images[MARGIN + block], preferred_element_type=F32)
    partial[...] = total.T
    for index in range(MARGIN):
        outer[index] = images[index].T
        outer[MARGIN + index] = images[MARGIN + blocks + index].T


def inner(
    total_blocks,
    first,
    lower_range,
    rot,
    coupling,
    lower_sizes,
    upper_sizes,
    lower,
    upper,
    dipole,
):
    slots, rows, states = lower.shape
    blocks, _, columns = upper.shape
    small = [in_hbm(a) for a in (lower_range, rot, coupling, lower_sizes, upper_sizes)]
    return pl.pallas_call(
        functools.partial(inner_kernel, total_blocks),
        out_shape=(
            pltpu.VMEM((2 * MARGIN, states, rows), BF16),
            pltpu.VMEM((states, columns), F32),
        ),
        in_specs=[smem_spec() for _ in range(6)] + [any_spec() for _ in range(3)],
        out_specs=(vmem_spec(), vmem_spec()),
        scratch_shapes=[
            pltpu.VMEM((slots + 2 * MARGIN + 2, rows, states), BF16),
            pltpu.VMEM((3, rows, rows), BF16),
            pltpu.VMEM(lower.shape, BF16),
            pltpu.VMEM(upper.shape, BF16),
            pltpu.VMEM(dipole.shape, BF16),
            pltpu.SemaphoreType.DMA((slots // CHUNK + 2,)),
        ],
        compiler_params=pltpu.CompilerParams(vmem_limit_bytes=VMEM_BYTES),
        name="inner",
    )(first, *small, in_hbm(lower), in_hbm(upper), in_hbm(dipole))


def outer_kernel(low, high, images, partial, out):
    total = partial[...]
    margin = low.shape[0]
    for index in range(margin):
        total += jnp.dot(images[index], low[index], preferred_element_type=F32)
    for index in range(margin):
        total += jnp.dot(images[margin + index], high[index], preferred_element_type=F32)
    out[...] = total.reshape(out.shape).astype(out.dtype)


def outer(low, high, images, partial, parts):
    states, columns = partial.shape
    return pl.pallas_call(
        outer_kernel,
        out_shape=pltpu.VMEM((parts, states // parts, columns), BF16),
        in_specs=[vmem_spec() for _ in range(4)],
        out_specs=vmem_spec(),
        compiler_params=pltpu.CompilerParams(vmem_limit_bytes=VMEM_BYTES),
        name="outer",
    )(in_vmem(low), in_vmem(high), images, partial)


def square_kernel(received, strength, sums):
    moment = jnp.sum(received[...].astype(F32), axis=0)
    squared = moment * moment
    strength[...] = squared
    row = jnp.sum(squared.T, axis=0, keepdims=True) * (1.0 / NUP)
    sums[...] = jnp.broadcast_to(row[None], sums.shape)


def square(received, tiles):
    _, band, columns = received.shape
    return pl.pallas_call(
        square_kernel,
        out_shape=(
            pltpu.VMEM((band, columns), F32),
            pltpu.VMEM((tiles, 1, band), F32),
        ),
        in_specs=[vmem_spec()],
        out_specs=(vmem_spec(), vmem_spec()),
        name="square",
    )(in_vmem(received))


def shards(
    lower_vectors,
    upper_vectors,
    dipole_vib,
    rot_factor,
    coupling,
    lower_sizes,
    upper_sizes,
    lower_range,
):
    parts = lax.axis_size("basis")
    tiles = lax.axis_size("tile")
    blocks = upper_vectors.shape[0]
    first = (lax.axis_index("basis") * blocks).astype(jnp.int32).reshape(1)
    forward = [(i, (i + 1) % parts) for i in range(parts)]
    backward = [(target, source) for source, target in forward]
    last_blocks, first_blocks = edges(upper_sizes, upper_vectors)
    low = lax.ppermute(last_blocks, "basis", forward)
    high = lax.ppermute(first_blocks, "basis", backward)
    images, partial = inner(
        parts * blocks,
        first,
        lower_range,
        rot_factor.T,
        coupling.T,
        lower_sizes,
        upper_sizes,
        lower_vectors,
        upper_vectors,
        dipole_vib,
    )
    mine = outer(low, high, images, partial, parts)
    received = lax.all_to_all(mine, "basis", 0, 0, tiled=True)
    strength, sums = square(received, tiles)
    gathered = lax.all_to_all(sums, "tile", 0, 0, tiled=True)
    average = jnp.sum(gathered[:, 0, :], axis=0)
    return (strength, average)


def solution(mesh):
    in_specs = (
        P("basis", None, None),
        P("basis", None, "tile"),
        P(),
        P("basis", None),
        P("basis", None),
        P("basis"),
        P("basis"),
        P("basis", None),
    )
    out_specs = (P("basis", "tile"), P("basis"))
    return jax.shard_map(shards, mesh=mesh, in_specs=in_specs, out_specs=out_specs, check_vma=False)
```

```python
import functools

import jax
import jax.numpy as jnp
from jax import lax
from jax.experimental import pallas as pl
from jax.experimental.pallas import tpu as pltpu
from jax.sharding import PartitionSpec as P

NUP = 1024
SHIFT = 8
MARGIN = SHIFT + 1
CHUNK = 12
AHEAD = 2
LEAST = 128
VMEM_BYTES = 28 * 1024 * 1024
BF16 = jnp.bfloat16
F32 = jnp.float32


def vmem_spec():
    return pl.BlockSpec(memory_space=pltpu.VMEM)


def smem_spec():
    return pl.BlockSpec(memory_space=pltpu.SMEM)


def any_spec():
    return pl.BlockSpec(memory_space=pl.ANY)


def in_hbm(array):
    return pltpu.with_memory_space_constraint(array, pltpu.HBM)


def in_vmem(array):
    return pltpu.with_memory_space_constraint(array, pltpu.VMEM)


def edges_kernel(sizes_hbm, upper, low, high, sizes, sems):
    blocks, rows, columns = upper.shape
    margin = low.shape[0]
    copies = [
        pltpu.make_async_copy(upper.at[pl.ds(blocks - margin, margin)], low, sems.at[0]),
        pltpu.make_async_copy(upper.at[pl.ds(0, margin)], high, sems.at[1]),
    ]
    known = pltpu.make_async_copy(sizes_hbm, sizes, sems.at[2])
    known.start()
    for copy in copies:
        copy.start()
    row_ids = LEAST + lax.broadcasted_iota(jnp.int32, (rows - LEAST, columns), 0)
    known.wait()
    for copy, out, first in zip(copies, (low, high), (blocks - margin, 0)):
        copy.wait()
        for block in range(margin):
            out[block, LEAST:] = jnp.where(
                row_ids < sizes[first + block], out[block, LEAST:], jnp.zeros((), BF16)
            )


def edges(upper_sizes, upper_vectors):
    blocks, rows, columns = upper_vectors.shape
    shape = pltpu.VMEM((MARGIN, rows, columns), BF16)
    return pl.pallas_call(
        edges_kernel,
        out_shape=(shape, shape),
        in_specs=[any_spec(), any_spec()],
        out_specs=(vmem_spec(), vmem_spec()),
        scratch_shapes=[
            pltpu.SMEM((blocks,), jnp.int32),
            pltpu.SemaphoreType.DMA((3,)),
        ],
        name="edges",
    )(in_hbm(upper_sizes), in_hbm(upper_vectors))


def masked(block, size):
    rows, columns = block.shape
    row_ids = LEAST + lax.broadcasted_iota(jnp.int32, (rows - LEAST, columns), 0)
    tail = jnp.where(row_ids < size, block[LEAST:], jnp.zeros((), BF16))
    return jnp.concatenate([block[:LEAST], tail], axis=0)


def inner_kernel(
    total_blocks,
    first_ref,
    range_ref,
    rot,
    coupling,
    lower_sizes,
    upper_sizes,
    lower_hbm,
    upper_hbm,
    dipole_hbm,
    above,
    below,
    partial,
    images,
    turned,
    lower,
    upper,
    dipole,
    sems,
):
    slots, rows, states = lower.shape
    blocks, _, columns = upper.shape
    start = range_ref[0, 0]
    count = range_ref[0, 1] - start
    base = start - first_ref[0] + MARGIN
    chunks = slots // CHUNK
    copies = [
        pltpu.make_async_copy(
            lower_hbm.at[pl.ds(chunk * CHUNK, CHUNK)],
            lower.at[pl.ds(chunk * CHUNK, CHUNK)],
            sems.at[chunk],
        )
        for chunk in range(chunks)
    ]
    copies.append(pltpu.make_async_copy(upper_hbm, upper, sems.at[chunks]))
    first_copy = pltpu.make_async_copy(dipole_hbm, dipole, sems.at[chunks + 1])
    first_copy.start()
    for copy in copies[:AHEAD]:
        copy.start()
    for index in range(2 * MARGIN):
        images[index] = jnp.zeros((rows, states), BF16)
    first_copy.wait()
    for d in range(3):
        turned[d] = dipole[d].T
    nearer = jnp.zeros((rows, states), F32)
    further = jnp.zeros((rows, states), F32)
    for slot in range(slots):
        if slot % CHUNK == 0:
            chunk = slot // CHUNK
            copies[chunk].wait()
            if chunk + AHEAD < len(copies):
                copies[chunk + AHEAD].start()
        live = masked(lower[slot], lower_sizes[slot])
        parts = []
        for d in range(3):
            factor = rot[d, slot] * coupling[d, slot].astype(F32)
            target = start + (slot + d - 1)
            there = (slot < count) & (target >= 0) & (target < total_blocks)
            factor = jnp.where(there, factor, 0.0)
            parts.append(factor * jnp.dot(turned[d], live, preferred_element_type=F32))
        images[base + (slot - 1)] = (nearer + parts[0]).astype(BF16)
        nearer = further + parts[1]
        further = parts[2]
    images[base + (slots - 1)] = nearer.astype(BF16)
    images[base + slots] = further.astype(BF16)
    for chunk in range(chunks, len(copies)):
        copies[chunk].wait()
    total = jnp.zeros((columns, states), F32)
    for block in range(blocks):
        live = masked(upper[block], upper_sizes[block])
        total += jnp.dot(live.T, images[MARGIN + block], preferred_element_type=F32)
    partial[...] = total.T
    for index in range(MARGIN):
        below[index] = images[index].T
        above[index] = images[MARGIN + blocks + index].T


def inner(
    total_blocks,
    first,
    lower_range,
    rot,
    coupling,
    lower_sizes,
    upper_sizes,
    lower,
    upper,
    dipole,
):
    slots, rows, states = lower.shape
    blocks, _, columns = upper.shape
    small = [in_hbm(a) for a in (lower_range, rot, coupling, lower_sizes, upper_sizes)]
    return pl.pallas_call(
        functools.partial(inner_kernel, total_blocks),
        out_shape=(
            pltpu.VMEM((MARGIN, states, rows), BF16),
            pltpu.VMEM((MARGIN, states, rows), BF16),
            pltpu.VMEM((states, columns), F32),
        ),
        in_specs=[smem_spec() for _ in range(6)] + [any_spec() for _ in range(3)],
        out_specs=(vmem_spec(), vmem_spec(), vmem_spec()),
        scratch_shapes=[
            pltpu.VMEM((slots + 2 * MARGIN + 2, rows, states), BF16),
            pltpu.VMEM((3, rows, rows), BF16),
            pltpu.VMEM(lower.shape, BF16),
            pltpu.VMEM(upper.shape, BF16),
            pltpu.VMEM(dipole.shape, BF16),
            pltpu.SemaphoreType.DMA((slots // CHUNK + 2,)),
        ],
        compiler_params=pltpu.CompilerParams(vmem_limit_bytes=VMEM_BYTES),
        name="inner",
    )(first, *small, in_hbm(lower), in_hbm(upper), in_hbm(dipole))


def outer_kernel(halo, images, partial, out):
    total = partial[...]
    for index in range(halo.shape[0]):
        total += jnp.dot(images[index], halo[index], preferred_element_type=F32)
    out[...] = total.reshape(out.shape).astype(out.dtype)


def outer(halo, images, partial, shape, dtype):
    return pl.pallas_call(
        outer_kernel,
        out_shape=pltpu.VMEM(shape, dtype),
        in_specs=[vmem_spec() for _ in range(3)],
        out_specs=vmem_spec(),
        compiler_params=pltpu.CompilerParams(vmem_limit_bytes=VMEM_BYTES),
        name="outer",
    )(in_vmem(halo), images, partial)


def square_kernel(received, strength, sums):
    moment = jnp.sum(received[...].astype(F32), axis=0)
    squared = moment * moment
    strength[...] = squared
    row = jnp.sum(squared.T, axis=0, keepdims=True) * (1.0 / NUP)
    sums[...] = row


def square(received):
    _, band, columns = received.shape
    return pl.pallas_call(
        square_kernel,
        out_shape=(
            pltpu.VMEM((band, columns), F32),
            pltpu.VMEM((1, band), F32),
        ),
        in_specs=[vmem_spec()],
        out_specs=(vmem_spec(), vmem_spec()),
        name="square",
    )(in_vmem(received))


def shards(
    lower_vectors,
    upper_vectors,
    dipole_vib,
    rot_factor,
    coupling,
    lower_sizes,
    upper_sizes,
    lower_range,
):
    parts = lax.axis_size("basis")
    tiles = lax.axis_size("tile")
    blocks = upper_vectors.shape[0]
    first = (lax.axis_index("basis") * blocks).astype(jnp.int32).reshape(1)
    forward = [(i, (i + 1) % parts) for i in range(parts)]
    backward = [(target, source) for source, target in forward]
    last_blocks, first_blocks = edges(upper_sizes, upper_vectors)
    low = lax.ppermute(last_blocks, "basis", forward)
    high = lax.ppermute(first_blocks, "basis", backward)
    above, below, partial = inner(
        parts * blocks,
        first,
        lower_range,
        rot_factor.T,
        coupling.T,
        lower_sizes,
        upper_sizes,
        lower_vectors,
        upper_vectors,
        dipole_vib,
    )
    partial = outer(low, below, partial, partial.shape, F32)
    states, columns = partial.shape
    mine = outer(high, above, partial, (parts, states // parts, columns), BF16)
    received = lax.all_to_all(mine, "basis", 0, 0, tiled=True)
    strength, sums = square(received)
    sums = sums + lax.ppermute(sums, "tile", [(i, i ^ 1) for i in range(tiles)])
    others = [
        lax.ppermute(sums, "tile", [(i, (i + step) % tiles) for i in range(tiles)])
        for step in range(2, tiles, 2)
    ]
    average = ((others[0] + others[2]) + (sums + others[1]))[0]
    return (strength, average)


def solution(mesh):
    in_specs = (
        P("basis", None, None),
        P("basis", None, "tile"),
        P(),
        P("basis", None),
        P("basis", None),
        P("basis"),
        P("basis"),
        P("basis", None),
    )
    out_specs = (P("basis", "tile"), P("basis"))
    return jax.shard_map(shards, mesh=mesh, in_specs=in_specs, out_specs=out_specs, check_vma=False)
```

```python
import functools

import jax
import jax.numpy as jnp
from jax import lax
from jax.experimental import pallas as pl
from jax.experimental.pallas import tpu as pltpu
from jax.sharding import PartitionSpec as P

NUP = 1024
SHIFT = 8
MARGIN = SHIFT + 1
CHUNK = 12
AHEAD = 2
LEAST = 128
VMEM_BYTES = 28 * 1024 * 1024
BF16 = jnp.bfloat16
F32 = jnp.float32


def vmem_spec():
    return pl.BlockSpec(memory_space=pltpu.VMEM)


def smem_spec():
    return pl.BlockSpec(memory_space=pltpu.SMEM)


def any_spec():
    return pl.BlockSpec(memory_space=pl.ANY)


def in_hbm(array):
    return pltpu.with_memory_space_constraint(array, pltpu.HBM)


def in_vmem(array):
    return pltpu.with_memory_space_constraint(array, pltpu.VMEM)


def even():
    return lax.rem(lax.axis_index("basis"), 2) == 0


def edges_kernel(sizes_hbm, upper, inward, outward, sizes, sems):
    blocks, rows, columns = upper.shape
    margin = inward.shape[0]
    firsts = [
        jnp.where(even(), blocks - margin, 0),
        jnp.where(even(), 0, blocks - margin),
    ]
    copies = [
        pltpu.make_async_copy(upper.at[pl.ds(first, margin)], out, sems.at[index])
        for index, (first, out) in enumerate(zip(firsts, (inward, outward)))
    ]
    known = pltpu.make_async_copy(sizes_hbm, sizes, sems.at[2])
    known.start()
    for copy in copies:
        copy.start()
    row_ids = LEAST + lax.broadcasted_iota(jnp.int32, (rows - LEAST, columns), 0)
    known.wait()
    for copy, out, first in zip(copies, (inward, outward), firsts):
        copy.wait()
        for block in range(margin):
            out[block, LEAST:] = jnp.where(
                row_ids < sizes[first + block], out[block, LEAST:], jnp.zeros((), BF16)
            )


def edges(upper_sizes, upper_vectors):
    blocks, rows, columns = upper_vectors.shape
    shape = pltpu.VMEM((MARGIN, rows, columns), BF16)
    return pl.pallas_call(
        edges_kernel,
        out_shape=(shape, shape),
        in_specs=[any_spec(), any_spec()],
        out_specs=(vmem_spec(), vmem_spec()),
        scratch_shapes=[
            pltpu.SMEM((blocks,), jnp.int32),
            pltpu.SemaphoreType.DMA((3,)),
        ],
        name="edges",
    )(in_hbm(upper_sizes), in_hbm(upper_vectors))


def masked(block, size):
    rows, columns = block.shape
    row_ids = LEAST + lax.broadcasted_iota(jnp.int32, (rows - LEAST, columns), 0)
    tail = jnp.where(row_ids < size, block[LEAST:], jnp.zeros((), BF16))
    return jnp.concatenate([block[:LEAST], tail], axis=0)


def inner_kernel(
    total_blocks,
    range_ref,
    rot,
    coupling,
    lower_sizes,
    upper_sizes,
    lower_hbm,
    upper_hbm,
    dipole_hbm,
    inward,
    outward,
    partial,
    images,
    turned,
    lower,
    upper,
    dipole,
    sems,
):
    slots, rows, states = lower.shape
    blocks, _, columns = upper.shape
    start = range_ref[0, 0]
    count = range_ref[0, 1] - start
    base = start - lax.axis_index("basis") * blocks + MARGIN
    chunks = slots // CHUNK
    copies = [
        pltpu.make_async_copy(
            lower_hbm.at[pl.ds(chunk * CHUNK, CHUNK)],
            lower.at[pl.ds(chunk * CHUNK, CHUNK)],
            sems.at[chunk],
        )
        for chunk in range(chunks)
    ]
    copies.append(pltpu.make_async_copy(upper_hbm, upper, sems.at[chunks]))
    first_copy = pltpu.make_async_copy(dipole_hbm, dipole, sems.at[chunks + 1])
    first_copy.start()
    for copy in copies[:AHEAD]:
        copy.start()
    for index in range(2 * MARGIN):
        images[index] = jnp.zeros((rows, states), BF16)
    first_copy.wait()
    for d in range(3):
        turned[d] = dipole[d].T
    nearer = jnp.zeros((rows, states), F32)
    further = jnp.zeros((rows, states), F32)
    for slot in range(slots):
        if slot % CHUNK == 0:
            chunk = slot // CHUNK
            copies[chunk].wait()
            if chunk + AHEAD < len(copies):
                copies[chunk + AHEAD].start()
        live = masked(lower[slot], lower_sizes[slot])
        parts = []
        for d in range(3):
            factor = rot[d, slot] * coupling[d, slot].astype(F32)
            target = start + (slot + d - 1)
            there = (slot < count) & (target >= 0) & (target < total_blocks)
            factor = jnp.where(there, factor, 0.0)
            parts.append(factor * jnp.dot(turned[d], live, preferred_element_type=F32))
        images[base + (slot - 1)] = (nearer + parts[0]).astype(BF16)
        nearer = further + parts[1]
        further = parts[2]
    images[base + (slots - 1)] = nearer.astype(BF16)
    images[base + slots] = further.astype(BF16)
    for chunk in range(chunks, len(copies)):
        copies[chunk].wait()
    total = jnp.zeros((columns, states), F32)
    for block in range(blocks):
        live = masked(upper[block], upper_sizes[block])
        total += jnp.dot(live.T, images[MARGIN + block], preferred_element_type=F32)
    partial[...] = total.T
    low, high = 0, MARGIN + blocks
    for index in range(MARGIN):
        inward[index] = images[jnp.where(even(), high, low) + index].T
        outward[index] = images[jnp.where(even(), low, high) + index].T


def inner(
    total_blocks,
    lower_range,
    rot,
    coupling,
    lower_sizes,
    upper_sizes,
    lower,
    upper,
    dipole,
):
    slots, rows, states = lower.shape
    blocks, _, columns = upper.shape
    small = [in_hbm(a) for a in (lower_range, rot, coupling, lower_sizes, upper_sizes)]
    return pl.pallas_call(
        functools.partial(inner_kernel, total_blocks),
        out_shape=(
            pltpu.VMEM((MARGIN, states, rows), BF16),
            pltpu.VMEM((MARGIN, states, rows), BF16),
            pltpu.VMEM((states, columns), F32),
        ),
        in_specs=[smem_spec() for _ in range(5)] + [any_spec() for _ in range(3)],
        out_specs=(vmem_spec(), vmem_spec(), vmem_spec()),
        scratch_shapes=[
            pltpu.VMEM((slots + 2 * MARGIN + 2, rows, states), BF16),
            pltpu.VMEM((3, rows, rows), BF16),
            pltpu.VMEM(lower.shape, BF16),
            pltpu.VMEM(upper.shape, BF16),
            pltpu.VMEM(dipole.shape, BF16),
            pltpu.SemaphoreType.DMA((slots // CHUNK + 2,)),
        ],
        compiler_params=pltpu.CompilerParams(vmem_limit_bytes=VMEM_BYTES),
        name="inner",
    )(*small, in_hbm(lower), in_hbm(upper), in_hbm(dipole))


def outer_kernel(halo, images, partial, out):
    total = partial[...]
    for index in range(halo.shape[0]):
        total += jnp.dot(images[index], halo[index], preferred_element_type=F32)
    out[...] = total.reshape(out.shape).astype(out.dtype)


def outer(halo, images, partial, shape, dtype):
    return pl.pallas_call(
        outer_kernel,
        out_shape=pltpu.VMEM(shape, dtype),
        in_specs=[vmem_spec() for _ in range(3)],
        out_specs=vmem_spec(),
        compiler_params=pltpu.CompilerParams(vmem_limit_bytes=VMEM_BYTES),
        name="outer",
    )(in_vmem(halo), images, partial)


def square_kernel(received, strength, sums):
    moment = jnp.sum(received[...].astype(F32), axis=0)
    squared = moment * moment
    strength[...] = squared
    row = jnp.sum(squared.T, axis=0, keepdims=True) * (1.0 / NUP)
    sums[...] = row


def square(received):
    _, band, columns = received.shape
    return pl.pallas_call(
        square_kernel,
        out_shape=(
            jax.ShapeDtypeStruct((band, columns), F32),
            pltpu.VMEM((1, band), F32),
        ),
        in_specs=[vmem_spec()],
        out_specs=(vmem_spec(), vmem_spec()),
        name="square",
    )(in_vmem(received))


def shards(
    lower_vectors,
    upper_vectors,
    dipole_vib,
    rot_factor,
    coupling,
    lower_sizes,
    upper_sizes,
    lower_range,
):
    parts = lax.axis_size("basis")
    tiles = lax.axis_size("tile")
    blocks = upper_vectors.shape[0]
    pairs = [(i, i ^ 1) for i in range(parts)]
    others = []
    for i in range(parts):
        other = ((i + 1) ^ 1) - 1
        for tile in range(tiles):
            there = (other, tile) if 0 <= other < parts else (i, tile ^ 1)
            others.append((i * tiles + tile, there[0] * tiles + there[1]))
    inward_blocks, outward_blocks = edges(upper_sizes, upper_vectors)
    inward_halo = lax.ppermute(inward_blocks, "basis", pairs)
    outward_halo = lax.ppermute(outward_blocks, ("basis", "tile"), others)
    inward, outward, partial = inner(
        parts * blocks,
        lower_range,
        rot_factor.T,
        coupling.T,
        lower_sizes,
        upper_sizes,
        lower_vectors,
        upper_vectors,
        dipole_vib,
    )
    partial = outer(inward_halo, inward, partial, partial.shape, F32)
    states, columns = partial.shape
    mine = outer(outward_halo, outward, partial, (parts, states // parts, columns), BF16)
    received = lax.all_to_all(mine, "basis", 0, 0, tiled=True)
    strength, sums = square(received)
    sums = sums + lax.ppermute(sums, "tile", [(i, i ^ 1) for i in range(tiles)])
    others = [
        lax.ppermute(sums, "tile", [(i, (i + step) % tiles) for i in range(tiles)])
        for step in range(2, tiles, 2)
    ]
    average = ((others[0] + others[2]) + (sums + others[1]))[0]
    return (strength, average)


def solution(mesh):
    in_specs = (
        P("basis", None, None),
        P("basis", None, "tile"),
        P(),
        P("basis", None),
        P("basis", None),
        P("basis"),
        P("basis"),
        P("basis", None),
    )
    out_specs = (P("basis", "tile"), P("basis"))
    return jax.shard_map(shards, mesh=mesh, in_specs=in_specs, out_specs=out_specs, check_vma=False)
```
